32 devices in a mesh: dp: 4 (over z), ctx: 4 (over x, core), tp: 2 (over y).
Axes of the slice: x: 2, y: 2, z: 4, core: 2. Of those that a mesh axis runs over, the one named last changes fastest.
Arguments:
- projected: bfloat16 [4, 3, 4096, 1024], P('dp', None, 'tp', 'ctx'), may hold values from -6 to 6
- cotangent: bfloat16 [4, 4096, 1024], P('dp', None, ('ctx', 'tp')), may hold values from -6 to 6
- short_filter: float32 [3, 3, 4096], P(None, None, 'tp'), may hold values from -3 to 3
- residues: float32 [4096, 16], P('tp'), may hold values from -3 to 3
- decay_rate: float32 [4096, 16], P('tp'), may hold values from 0.00024414062 to 0.035
- skip_gain: float32 [4096], P('tp'), may hold values from -1 to 1
Outputs:
- hyena_out: bfloat16 [4, 4096, 1024], P('dp', 'tp', 'ctx')
- input_grad: bfloat16 [4, 3, 4096, 1024], P('dp', None, 'tp', 'ctx')
- residue_grad: float32 [4096, 16], P('tp')
- skip_grad: float32 [4096], P('tp')
The draws below stay inside these ranges and needn't reach their ends.
All inputs are finite; a program needn't handle non-finite values.
Results may differ from the reference program's by a relative error of at most 0.0076.
Values may be sent and summed in bfloat16 or wider, within the bound.
A program may use at most 128 MiB of HBM per device.

```python
import math
import jax
import jax.numpy as jnp
from jax import lax

D = 4096
ORDER = 16
SHORT = 3
SEQ = 1024
SAMPLES = 4


def block_levels(own_key, dims, cuts, low, top_value):
    def one(dim, shards_of):
        draws = jax.random.uniform(jax.random.fold_in(jax.random.fold_in(own_key, 6), dim), (shards_of,), jnp.float32, low / len(cuts), top_value / len(cuts))
        return jnp.repeat(jnp.exp(draws), dims[dim] // shards_of).reshape((-1,) + (1,) * (len(dims) - dim - 1))

    level = one(*cuts[0])
    for cut in cuts[1:]:
        level = level * one(*cut)
    return level


def bell_draw(stream_key, shape, width, most, split=(), held_as=jnp.bfloat16):
    entries = jax.random.normal(stream_key, shape, jnp.float32) * width
    if len(split) > 0:
        entries = block_levels(stream_key, shape, split, -0.22, 0.18) * entries
    return jnp.clip(entries, min=-most, max=most).astype(held_as)


def setup_inputs(seed: int = 0) -> dict:
    arg_keys = jax.random.split(jax.random.key(seed), 7)
    return {
        "projected": bell_draw(arg_keys[0], (SAMPLES, 3, D, SEQ), 1.0, 6.0, ((0, 4), (2, 2), (3, 4))),
        "cotangent": bell_draw(arg_keys[1], (SAMPLES, D, SEQ), 1.0, 6.0, ((0, 4), (2, 8))),
        "short_filter": bell_draw(arg_keys[2], (3, SHORT, D), 0.6, 3.0, ((2, 2),), jnp.float32),
        "residues": bell_draw(arg_keys[3], (D, ORDER), 0.35, 3.0, ((0, 2),), jnp.float32),
        "decay_rate": jnp.clip(jnp.exp(math.log(0.035) - 4.96535895 * jax.random.uniform(arg_keys[4], (D, ORDER), jnp.float32) ** block_levels(arg_keys[4], (D, ORDER), ((0, 2),), -0.2, 0.2)), 0.00024414062, 0.035),
        "skip_gain": jnp.clip(jax.random.uniform(arg_keys[5], (D,), jnp.float32, -1.0, 1.0) * block_levels(arg_keys[5], (D,), ((0, 2),), -0.4, 0.0), -1.0, 1.0),
    }


exact_mode = lax.Precision.HIGHEST

def rounded(values):
    return lax.optimization_barrier(values.astype(jnp.bfloat16)).astype(jnp.float32)

def causal_taps(signal, tap_weights):
    length = signal.shape[2]
    result = tap_weights[:, 0, :, None] * signal
    for lag_index in range(1, SHORT):
        shifted = jnp.pad(signal, ((0, 0), (0, 0), (lag_index, 0)))[:, :, :length]
        result = result + tap_weights[:, lag_index, :, None] * shifted
    return result

def anticausal_taps(signal, tap_weights):
    result = tap_weights[:, 0, :, None] * signal
    for lag_index in range(1, SHORT):
        shifted = jnp.pad(signal, ((0, 0), (0, 0), (0, lag_index)))[:, :, lag_index:]
        result = result + tap_weights[:, lag_index, :, None] * shifted
    return result

def long_block(group_items):
    product, adjoint, rate_rows, residue_rows, gain_rows = group_items
    length = product.shape[1]
    lag_values = jnp.arange(length).astype(rate_rows.dtype)
    falloff = jnp.exp(-rate_rows[:, :, None] * lag_values)
    root_rate = jnp.sqrt(2.0 * rate_rows)
    kernel = jnp.einsum('cn,cnl->cl', residue_rows * root_rate, falloff, precision=exact_mode)
    padded = 2 * length
    product_freq = jnp.fft.rfft(product, padded, axis=1)
    adjoint_freq = jnp.fft.rfft(adjoint, padded, axis=1)
    kernel_freq = jnp.fft.rfft(kernel, padded, axis=1)
    forward = jnp.fft.irfft(product_freq * kernel_freq, padded, axis=1)[:, :length]
    forward = forward + gain_rows[:, None] * product
    backward = jnp.fft.irfft(adjoint_freq * jnp.conj(kernel_freq), padded, axis=1)[:, :length]
    backward = backward + gain_rows[:, None] * adjoint
    lagged = jnp.fft.irfft(adjoint_freq * jnp.conj(product_freq), padded, axis=1)[:, :length]
    mode_raw = root_rate * jnp.einsum('cl,cnl->cn', lagged, falloff, precision=exact_mode)
    skip_raw = lax.optimization_barrier(jnp.sum(adjoint * product, axis=1))
    return (forward.astype(jnp.bfloat16), backward.astype(jnp.bfloat16), mode_raw, skip_raw)

def reference(projected, cotangent, short_filter, residues, decay_rate, skip_gain):
    block_total = D // 64

    def one_sample(sample_items):
        proj_rows, grad_rows = sample_items
        featured = rounded(causal_taps(proj_rows.astype(jnp.float32), short_filter))
        query_feat = featured[0]
        key_feat = featured[1]
        value_feat = featured[2]
        product = rounded(key_feat * value_feat)
        grad_out = grad_rows.astype(jnp.float32)
        adjoint = rounded(grad_out * query_feat)
        stacked = (product.reshape(block_total, 64, SEQ), adjoint.reshape(block_total, 64, SEQ), decay_rate.reshape(block_total, 64, ORDER), residues.reshape(block_total, 64, ORDER), skip_gain.reshape(block_total, 64))
        forward, backward, mode_raw, skip_raw = lax.map(long_block, stacked)
        forward = forward.reshape(D, SEQ).astype(jnp.float32)
        backward = backward.reshape(D, SEQ).astype(jnp.float32)
        hyena_out = (query_feat * forward).astype(jnp.bfloat16)
        feature_grad = rounded(jnp.stack([grad_out * forward, backward * value_feat, backward * key_feat]))
        input_grad = anticausal_taps(feature_grad, short_filter).astype(jnp.bfloat16)
        return (hyena_out, input_grad, mode_raw.reshape(D, ORDER), skip_raw.reshape(D))
    outputs = lax.map(one_sample, (projected, cotangent))
    grad_scale = 1.0 / jnp.sqrt(jnp.asarray(SEQ * SAMPLES, dtype=residues.dtype))
    residue_grad = lax.optimization_barrier(jnp.sum(outputs[2], axis=0)) * grad_scale
    skip_grad = lax.optimization_barrier(jnp.sum(outputs[3], axis=0)) * grad_scale
    return (outputs[0], outputs[1], residue_grad, skip_grad)
```

```python
import math

import jax
import jax.numpy as jnp
from jax import lax
from jax.experimental import pallas as pl
from jax.experimental.pallas import tpu as pltpu
from jax.sharding import PartitionSpec as P

LANES = 128
SUBS = 8
F32 = jnp.float32
BF16 = jnp.bfloat16


def rounded(values):
    return values.astype(BF16).astype(F32)


def nt_dot(left, right):
    return lax.dot_general(left, right, (((1,), (1,)), ((), ())), preferred_element_type=F32)


def row_of(ref, index):
    return jnp.broadcast_to(ref[index : index + 1, :], (SUBS, LANES))


def tree_sum(terms):
    terms = list(terms)
    while len(terms) > 1:
        paired = [terms[i] + terms[i + 1] for i in range(0, len(terms) - 1, 2)]
        if len(terms) % 2:
            paired.append(terms[-1])
        terms = paired
    return terms[0]


def sublane_ids():
    return lax.broadcasted_iota(jnp.int32, (SUBS, LANES), 0)


def scan_subs(ends, rate, span, sub, backward):
    running = ends
    step = 1
    while step < SUBS:
        if backward:
            moved = jnp.where(sub < SUBS - step, pltpu.roll(running, SUBS - step, 0), 0.0)
        else:
            moved = jnp.where(sub >= step, pltpu.roll(running, step, 0), 0.0)
        running = running + jnp.exp(-rate * float(span * step)) * moved
        step *= 2
    if backward:
        before = jnp.where(sub < SUBS - 1, pltpu.roll(running, SUBS - 1, 0), 0.0)
    else:
        before = jnp.where(sub >= 1, pltpu.roll(running, 1, 0), 0.0)
    return before, running


def first_kernel(proj, cot, rim, taps, rate, perm, feat, inner, totals, edge, u_s, d_s):
    order = rate.shape[0]
    tokens = proj.shape[2]
    span = tokens // SUBS
    sub = sublane_ids()
    streams = []
    for s in range(3):
        rows = nt_dot(perm[...], proj[s])
        last = jnp.where(
            sub == 0, row_of(rim, 2 * s + 1), pltpu.roll(rows[tokens - SUBS :], 1, 0)
        )
        prior = jnp.where(
            sub == 0,
            row_of(rim, 2 * s),
            pltpu.roll(rows[tokens - 2 * SUBS : tokens - SUBS], 1, 0),
        )
        wide = jnp.concatenate([prior, last, rows], axis=0)
        made = taps[3 * s : 3 * s + 1, :] * rows
        made = made + taps[3 * s + 1 : 3 * s + 2, :] * wide[SUBS : SUBS + tokens]
        made = made + taps[3 * s + 2 : 3 * s + 3, :] * wide[:tokens]
        narrow = made.astype(BF16)
        feat[s] = narrow
        streams.append(narrow.astype(F32))
    pieces, part = cot.shape[0], cot.shape[2]
    grad = nt_dot(perm[:, :part], cot[0])
    for p in range(1, pieces):
        grad = grad + nt_dot(perm[:, p * part : (p + 1) * part], cot[p])
    feat[3] = grad.astype(BF16)
    streams.append(grad)
    for s in range(4):
        edge[2 * s : 2 * s + 1, :] = streams[s][0:1]
        edge[2 * s + 1 : 2 * s + 2, :] = streams[s][SUBS : SUBS + 1]
    u_s[...] = rounded(streams[1] * streams[2])
    d_s[...] = rounded(streams[3] * streams[0])
    falls = [jnp.exp(-row_of(rate, n)) for n in range(order)]

    def body(j, carry):
        ahead, back = carry
        uj = u_s[pl.ds(pl.multiple_of(j * SUBS, SUBS), SUBS), :]
        dj = d_s[pl.ds(pl.multiple_of((span - 1 - j) * SUBS, SUBS), SUBS), :]
        ahead = tuple(falls[n] * ahead[n] + uj for n in range(order))
        back = tuple(falls[n] * back[n] + dj for n in range(order))
        return ahead, back

    zero = jnp.zeros((SUBS, LANES), F32)
    ahead, back = lax.fori_loop(0, span, body, ((zero,) * order, (zero,) * order), unroll=4)
    for n in range(order):
        rate_n = row_of(rate, n)
        before, running = scan_subs(ahead[n], rate_n, span, sub, False)
        inner[n * SUBS : (n + 1) * SUBS, :] = before
        totals[n : n + 1, :] = running[SUBS - 1 : SUBS]
        before, running = scan_subs(back[n], rate_n, span, sub, True)
        inner[(order + n) * SUBS : (order + n + 1) * SUBS, :] = before
        totals[order + n : order + n + 1, :] = running[0:1]


def second_kernel(
    scale, feat, inner, states, edge, taps, rate, res, gain, perm_t, ident,
    out, grad_in, sums, u_s, d_s, z_s, b_s, a_s, w_s, x_s,
):
    order = rate.shape[0]
    tokens = feat.shape[1]
    span = tokens // SUBS
    sub = sublane_ids()
    sub_f = sub.astype(F32)
    root = jnp.sqrt(2.0 * rate[...])
    weight = res[...] * root
    fall = jnp.exp(-rate[...])
    for n in range(order):
        a_s[n * SUBS : (n + 1) * SUBS, :] = jnp.broadcast_to(fall[n : n + 1], (SUBS, LANES))
        w_s[n * SUBS : (n + 1) * SUBS, :] = jnp.broadcast_to(weight[n : n + 1], (SUBS, LANES))
    gain_b = jnp.broadcast_to(gain[...], (SUBS, LANES))
    u_s[...] = rounded(feat[1].astype(F32) * feat[2].astype(F32))
    d_s[...] = rounded(feat[3].astype(F32) * feat[0].astype(F32))

    def mode(ref, n):
        return ref[n * SUBS : (n + 1) * SUBS, :]

    def ahead_body(j, carry):
        xs, gs, skip = carry
        at = pl.ds(pl.multiple_of(j * SUBS, SUBS), SUBS)
        uj, dj = u_s[at, :], d_s[at, :]
        xs = tuple(mode(a_s, n) * xs[n] + uj for n in range(order))
        gs = tuple(gs[n] + dj * xs[n] for n in range(order))
        y = tree_sum([mode(w_s, n) * xs[n] for n in range(order)])
        z_s[at, :] = rounded(y + gain_b * uj)
        return xs, gs, skip + dj * uj

    zero = jnp.zeros((SUBS, LANES), F32)
    start = tuple(
        mode(inner, n) + jnp.exp(-row_of(rate, n) * (sub_f * float(span))) * row_of(states, n)
        for n in range(order)
    )
    xs, gs, skip = lax.fori_loop(
        0, span, ahead_body, (start, (zero,) * order, zero), unroll=4
    )
    for n in range(order):
        sums[n : n + 1, :] = jnp.sum(gs[n], axis=0, keepdims=True)
        x_s[n : n + 1, :] = xs[n][SUBS - 1 : SUBS]
    sums[0:order, :] = sums[0:order, :] * root * scale
    sums[order : order + SUBS, :] = jnp.broadcast_to(
        jnp.sum(skip, axis=0, keepdims=True) * scale, (SUBS, LANES)
    )

    def back_body(i, xs):
        at = pl.ds(pl.multiple_of((span - 1 - i) * SUBS, SUBS), SUBS)
        dj = d_s[at, :]
        xs = tuple(mode(a_s, n) * xs[n] + dj for n in range(order))
        y = tree_sum([mode(w_s, n) * xs[n] for n in range(order)])
        b_s[at, :] = rounded(y + gain_b * dj)
        return xs

    start = tuple(
        mode(inner, order + n)
        + jnp.exp(-row_of(rate, n) * ((SUBS - 1.0 - sub_f) * float(span)))
        * row_of(states, order + n)
        for n in range(order)
    )
    lax.fori_loop(0, span, back_body, start, unroll=4)

    gain_r = gain[...]
    q_n, k_n, v_n, g_n = (
        [edge[2 * s : 2 * s + 1, :], edge[2 * s + 1 : 2 * s + 2, :]] for s in range(4)
    )
    u_n = [rounded(k_n[i] * v_n[i]) for i in range(2)]
    d_n = [rounded(g_n[i] * q_n[i]) for i in range(2)]
    state = x_s[...]
    b_state = states[order : 2 * order, :]
    next_rows = []
    for i in range(2):
        state = fall * state + u_n[i]
        z_n = rounded(jnp.sum(weight * state, axis=0, keepdims=True) + gain_r * u_n[i])
        if i:
            b_state = (b_state - d_n[i - 1]) / fall
        du_n = rounded(jnp.sum(weight * b_state, axis=0, keepdims=True) + gain_r * d_n[i])
        next_rows.append(
            [rounded(g_n[i] * z_n), rounded(du_n * v_n[i]), rounded(du_n * k_n[i])]
        )

    def send_out(rows):
        ordered = jnp.dot(perm_t[...], rows, preferred_element_type=F32).astype(BF16)
        return nt_dot(ident[...], ordered).astype(BF16)

    z = z_s[...]
    du = b_s[...]
    out[...] = send_out((feat[0].astype(F32) * z).astype(BF16))
    for s in range(3):
        if s == 0:
            rows = rounded(feat[3].astype(F32) * z)
        else:
            rows = rounded(du * feat[3 - s].astype(F32))
        after = [
            jnp.where(
                sub == SUBS - 1,
                jnp.broadcast_to(next_rows[i][s], (SUBS, LANES)),
                pltpu.roll(rows[i * SUBS : (i + 1) * SUBS], SUBS - 1, 0),
            )
            for i in range(2)
        ]
        wide = jnp.concatenate([rows] + after, axis=0)
        made = taps[3 * s : 3 * s + 1, :] * rows
        made = made + taps[3 * s + 1 : 3 * s + 2, :] * wide[SUBS : SUBS + tokens]
        made = made + taps[3 * s + 2 : 3 * s + 3, :] * wide[2 * SUBS :]
        grad_in[s] = send_out(made.astype(BF16))


def shifted(array, by):
    count = lax.axis_size("ctx")
    pairs = [(i, i + by) for i in range(count) if 0 <= i + by < count]
    return lax.ppermute(array, "ctx", pairs)


def entering(total, span_rate, first, sign):
    count = lax.axis_size("ctx")
    result, width = first, 1
    window = total + jnp.exp(-span_rate) * first
    reach = 2
    while width < count - 1:
        moved = shifted(window, sign * reach)
        result = result + jnp.exp(-span_rate * float(width)) * moved
        width += reach
        if width < count - 1:
            window = window + jnp.exp(-span_rate * float(reach)) * moved
        reach *= 2
    return result


def on_device(projected, cotangent, short_filter, residues, decay_rate, skip_gain):
    proj = projected[0]
    _, chans, tokens = proj.shape
    order = residues.shape[1]
    span = tokens // SUBS
    tiles = chans // LANES
    pieces = lax.axis_size("tp")
    total_tokens = tokens * lax.axis_size("ctx") * lax.axis_size("dp")
    scale = 1.0 / math.sqrt(total_tokens)

    cot = cotangent[0].reshape(pieces, chans, tokens // pieces)
    cot = lax.all_to_all(cot, "tp", split_axis=0, concat_axis=0, tiled=True)
    rim = jnp.swapaxes(proj[:, :, tokens - 2 :], 1, 2).reshape(6, chans)
    rim = shifted(rim, 1).astype(F32)
    taps = short_filter.reshape(9, chans)
    rate = decay_rate.T
    res = residues.T
    gain = skip_gain[None]
    r = jnp.arange(tokens)
    perm = ((r % SUBS) * span + r // SUBS)[:, None] == r[None, :]
    perm_t = perm.T.astype(BF16)
    perm = perm.astype(BF16)
    ident = jnp.eye(LANES, dtype=BF16)

    def cols(*lead):
        zeros = (0,) * len(lead)
        return pl.BlockSpec(lead + (LANES,), lambda i: zeros + (i,))

    def whole(rows, columns):
        return pl.BlockSpec((rows, columns), lambda i: (0, 0))

    def chan_rows(lead, last):
        return pl.BlockSpec((lead, LANES, last), lambda i: (0, i, 0))

    params = pltpu.CompilerParams(
        dimension_semantics=("arbitrary",), vmem_limit_bytes=40 * 2**20
    )
    work = chans * tokens * order
    feat, inner, totals, edge = pl.pallas_call(
        first_kernel,
        grid=(tiles,),
        in_specs=[
            chan_rows(3, tokens),
            chan_rows(pieces, tokens // pieces),
            cols(6),
            cols(9),
            cols(order),
            whole(tokens, tokens),
        ],
        out_specs=[cols(4, tokens), cols(2 * order * SUBS), cols(2 * order), cols(8)],
        out_shape=[
            jax.ShapeDtypeStruct((4, tokens, chans), BF16),
            jax.ShapeDtypeStruct((2 * order * SUBS, chans), F32),
            jax.ShapeDtypeStruct((2 * order, chans), F32),
            jax.ShapeDtypeStruct((8, chans), F32),
        ],
        scratch_shapes=[pltpu.VMEM((tokens, LANES), F32)] * 2,
        compiler_params=params,
        cost_estimate=pl.CostEstimate(
            flops=4 * work, bytes_accessed=2**23, transcendentals=0
        ),
    )(proj, cot, rim, taps, rate, perm)

    span_rate = rate * float(tokens)
    ahead, back = totals[:order], totals[order:]
    first_ahead = shifted(ahead, 1)
    first_back = shifted(jnp.concatenate([back, edge], axis=0), -1)
    next_edge = first_back[order:]
    states = jnp.concatenate(
        [
            entering(ahead, span_rate, first_ahead, 1),
            entering(back, span_rate, first_back[:order], -1),
        ],
        axis=0,
    )

    out, grad_in, sums = pl.pallas_call(
        lambda *refs: second_kernel(scale, *refs),
        grid=(tiles,),
        in_specs=[
            cols(4, tokens),
            cols(2 * order * SUBS),
            cols(2 * order),
            cols(8),
            cols(9),
            cols(order),
            cols(order),
            cols(1),
            whole(tokens, tokens),
            whole(LANES, LANES),
        ],
        out_specs=[
            pl.BlockSpec((LANES, tokens), lambda i: (i, 0)),
            chan_rows(3, tokens),
            cols(order + SUBS),
        ],
        out_shape=[
            jax.ShapeDtypeStruct((chans, tokens), BF16),
            jax.ShapeDtypeStruct((3, chans, tokens), BF16),
            jax.ShapeDtypeStruct((order + SUBS, chans), F32),
        ],
        scratch_shapes=[pltpu.VMEM((tokens, LANES), F32)] * 4
        + [pltpu.VMEM((order * SUBS, LANES), F32)] * 2
        + [pltpu.VMEM((order, LANES), F32)],
        compiler_params=params,
        cost_estimate=pl.CostEstimate(
            flops=12 * work, bytes_accessed=2**23, transcendentals=0
        ),
    )(feat, inner, states, next_edge, taps, rate, res, gain, perm_t, ident)
    sums = lax.psum(sums, ("dp", "ctx"))
    return (out[None], grad_in[None], sums[:order].T, sums[order])


def solution(mesh):
    placed = (
        P("dp", None, "tp", "ctx"),
        P("dp", None, ("ctx", "tp")),
        P(None, None, "tp"),
        P("tp", None),
        P("tp", None),
        P("tp"),
    )
    return jax.shard_map(
        on_device,
        mesh=mesh,
        in_specs=placed,
        out_specs=(P("dp", "tp", "ctx"), P("dp", None, "tp", "ctx"), P("tp", None), P("tp")),
        check_vma=False,
    )
```

```python
import math

import jax
import jax.numpy as jnp
from jax import lax
from jax.experimental import pallas as pl
from jax.experimental.pallas import tpu as pltpu
from jax.sharding import PartitionSpec as P

LANES = 128
SUBS = 8
F32 = jnp.float32
BF16 = jnp.bfloat16


def rounded(values):
    return values.astype(BF16).astype(F32)


def nt_dot(left, right):
    return lax.dot_general(left, right, (((1,), (1,)), ((), ())), preferred_element_type=F32)


def row_of(ref, index):
    return jnp.broadcast_to(ref[index : index + 1, :], (SUBS, LANES))


def tree_sum(terms):
    terms = list(terms)
    while len(terms) > 1:
        paired = [terms[i] + terms[i + 1] for i in range(0, len(terms) - 1, 2)]
        if len(terms) % 2:
            paired.append(terms[-1])
        terms = paired
    return terms[0]


def sublane_ids():
    return lax.broadcasted_iota(jnp.int32, (SUBS, LANES), 0)


def scan_subs(ends, rate, span, sub, backward):
    running = ends
    step = 1
    while step < SUBS:
        if backward:
            moved = jnp.where(sub < SUBS - step, pltpu.roll(running, SUBS - step, 0), 0.0)
        else:
            moved = jnp.where(sub >= step, pltpu.roll(running, step, 0), 0.0)
        running = running + jnp.exp(-rate * float(span * step)) * moved
        step *= 2
    if backward:
        before = jnp.where(sub < SUBS - 1, pltpu.roll(running, SUBS - 1, 0), 0.0)
    else:
        before = jnp.where(sub >= 1, pltpu.roll(running, 1, 0), 0.0)
    return before, running


def first_kernel(proj, cot, rim, taps, rate, perm, feat, inner, totals, edge, u_s, d_s):
    order = rate.shape[0]
    tokens = proj.shape[2]
    span = tokens // SUBS
    sub = sublane_ids()
    streams = []
    for s in range(3):
        rows = nt_dot(perm[...], proj[s])
        last = jnp.where(
            sub == 0, row_of(rim, 2 * s + 1), pltpu.roll(rows[tokens - SUBS :], 1, 0)
        )
        prior = jnp.where(
            sub == 0,
            row_of(rim, 2 * s),
            pltpu.roll(rows[tokens - 2 * SUBS : tokens - SUBS], 1, 0),
        )
        wide = jnp.concatenate([prior, last, rows], axis=0)
        made = taps[3 * s : 3 * s + 1, :] * rows
        made = made + taps[3 * s + 1 : 3 * s + 2, :] * wide[SUBS : SUBS + tokens]
        made = made + taps[3 * s + 2 : 3 * s + 3, :] * wide[:tokens]
        narrow = made.astype(BF16)
        feat[s] = narrow
        streams.append(narrow.astype(F32))
    pieces, part = cot.shape[0], cot.shape[2]
    grad = nt_dot(perm[:, :part], cot[0])
    for p in range(1, pieces):
        grad = grad + nt_dot(perm[:, p * part : (p + 1) * part], cot[p])
    feat[3] = grad.astype(BF16)
    streams.append(grad)
    for s in range(4):
        edge[2 * s : 2 * s + 1, :] = streams[s][0:1]
        edge[2 * s + 1 : 2 * s + 2, :] = streams[s][SUBS : SUBS + 1]
    u_s[...] = rounded(streams[1] * streams[2])
    d_s[...] = rounded(streams[3] * streams[0])
    falls = [jnp.exp(-row_of(rate, n)) for n in range(order)]

    def body(j, carry):
        ahead, back = carry
        uj = u_s[pl.ds(pl.multiple_of(j * SUBS, SUBS), SUBS), :]
        dj = d_s[pl.ds(pl.multiple_of((span - 1 - j) * SUBS, SUBS), SUBS), :]
        ahead = tuple(falls[n] * ahead[n] + uj for n in range(order))
        back = tuple(falls[n] * back[n] + dj for n in range(order))
        return ahead, back

    zero = jnp.zeros((SUBS, LANES), F32)
    ahead, back = lax.fori_loop(0, span, body, ((zero,) * order, (zero,) * order), unroll=4)
    for n in range(order):
        rate_n = row_of(rate, n)
        before, running = scan_subs(ahead[n], rate_n, span, sub, False)
        inner[n * SUBS : (n + 1) * SUBS, :] = before
        totals[n : n + 1, :] = running[SUBS - 1 : SUBS]
        before, running = scan_subs(back[n], rate_n, span, sub, True)
        inner[(order + n) * SUBS : (order + n + 1) * SUBS, :] = before
        totals[order + n : order + n + 1, :] = running[0:1]


def second_kernel(
    scale, feat, inner, states, edge, taps, rate, res, gain, perm_t, ident,
    out, grad_in, sums, u_s, d_s, z_s, b_s, a_s, w_s, x_s,
):
    order = rate.shape[0]
    tokens = feat.shape[1]
    span = tokens // SUBS
    sub = sublane_ids()
    sub_f = sub.astype(F32)
    root = jnp.sqrt(2.0 * rate[...])
    weight = res[...] * root
    fall = jnp.exp(-rate[...])
    for n in range(order):
        a_s[n * SUBS : (n + 1) * SUBS, :] = jnp.broadcast_to(fall[n : n + 1], (SUBS, LANES))
        w_s[n * SUBS : (n + 1) * SUBS, :] = jnp.broadcast_to(weight[n : n + 1], (SUBS, LANES))
    gain_b = jnp.broadcast_to(gain[...], (SUBS, LANES))
    u_s[...] = rounded(feat[1].astype(F32) * feat[2].astype(F32))
    d_s[...] = rounded(feat[3].astype(F32) * feat[0].astype(F32))

    def mode(ref, n):
        return ref[n * SUBS : (n + 1) * SUBS, :]

    def ahead_body(j, carry):
        xs, gs, skip = carry
        at = pl.ds(pl.multiple_of(j * SUBS, SUBS), SUBS)
        uj, dj = u_s[at, :], d_s[at, :]
        xs = tuple(mode(a_s, n) * xs[n] + uj for n in range(order))
        gs = tuple(gs[n] + dj * xs[n] for n in range(order))
        y = tree_sum([mode(w_s, n) * xs[n] for n in range(order)])
        z_s[at, :] = rounded(y + gain_b * uj)
        return xs, gs, skip + dj * uj

    zero = jnp.zeros((SUBS, LANES), F32)
    start = tuple(
        mode(inner, n) + jnp.exp(-row_of(rate, n) * (sub_f * float(span))) * row_of(states, n)
        for n in range(order)
    )
    xs, gs, skip = lax.fori_loop(
        0, span, ahead_body, (start, (zero,) * order, zero), unroll=4
    )
    for n in range(order):
        sums[n : n + 1, :] = jnp.sum(gs[n], axis=0, keepdims=True)
        x_s[n : n + 1, :] = xs[n][SUBS - 1 : SUBS]
    sums[0:order, :] = sums[0:order, :] * root * scale
    sums[order : order + SUBS, :] = jnp.broadcast_to(
        jnp.sum(skip, axis=0, keepdims=True) * scale, (SUBS, LANES)
    )

    def back_body(i, xs):
        at = pl.ds(pl.multiple_of((span - 1 - i) * SUBS, SUBS), SUBS)
        dj = d_s[at, :]
        xs = tuple(mode(a_s, n) * xs[n] + dj for n in range(order))
        y = tree_sum([mode(w_s, n) * xs[n] for n in range(order)])
        b_s[at, :] = rounded(y + gain_b * dj)
        return xs

    start = tuple(
        mode(inner, order + n)
        + jnp.exp(-row_of(rate, n) * ((SUBS - 1.0 - sub_f) * float(span)))
        * row_of(states, order + n)
        for n in range(order)
    )
    lax.fori_loop(0, span, back_body, start, unroll=4)

    gain_r = gain[...]
    q_n, k_n, v_n, g_n = (
        [edge[2 * s : 2 * s + 1, :], edge[2 * s + 1 : 2 * s + 2, :]] for s in range(4)
    )
    u_n = [rounded(k_n[i] * v_n[i]) for i in range(2)]
    d_n = [rounded(g_n[i] * q_n[i]) for i in range(2)]
    state = x_s[...]
    b_state = states[order : 2 * order, :]
    next_rows = []
    for i in range(2):
        state = fall * state + u_n[i]
        z_n = rounded(jnp.sum(weight * state, axis=0, keepdims=True) + gain_r * u_n[i])
        if i:
            b_state = (b_state - d_n[i - 1]) / fall
        du_n = rounded(jnp.sum(weight * b_state, axis=0, keepdims=True) + gain_r * d_n[i])
        next_rows.append(
            [rounded(g_n[i] * z_n), rounded(du_n * v_n[i]), rounded(du_n * k_n[i])]
        )

    def send_out(rows):
        ordered = jnp.dot(perm_t[...], rows, preferred_element_type=F32).astype(BF16)
        return nt_dot(ident[...], ordered).astype(BF16)

    z = z_s[...]
    du = b_s[...]
    out[...] = send_out((feat[0].astype(F32) * z).astype(BF16))
    for s in range(3):
        if s == 0:
            rows = rounded(feat[3].astype(F32) * z)
        else:
            rows = rounded(du * feat[3 - s].astype(F32))
        after = [
            jnp.where(
                sub == SUBS - 1,
                jnp.broadcast_to(next_rows[i][s], (SUBS, LANES)),
                pltpu.roll(rows[i * SUBS : (i + 1) * SUBS], SUBS - 1, 0),
            )
            for i in range(2)
        ]
        wide = jnp.concatenate([rows] + after, axis=0)
        made = taps[3 * s : 3 * s + 1, :] * rows
        made = made + taps[3 * s + 1 : 3 * s + 2, :] * wide[SUBS : SUBS + tokens]
        made = made + taps[3 * s + 2 : 3 * s + 3, :] * wide[2 * SUBS :]
        grad_in[s] = send_out(made.astype(BF16))


def shifted(array, by):
    count = lax.axis_size("ctx")
    pairs = [(i, i + by) for i in range(count) if 0 <= i + by < count]
    return lax.ppermute(array, "ctx", pairs)


MESH = pl.DeviceIdType.MESH


def exchange_kernel(count, totals, edge, rate, states, next_edge, held_a, held_b, held_e,
                    send_a, send_b, recv_a, recv_b, edge_sem):
    order = rate.shape[0]
    me = lax.axis_index("ctx")
    barrier = pltpu.get_barrier_semaphore()

    def greet(k, _):
        pl.semaphore_signal(
            barrier, inc=1, device_id={"ctx": lax.rem(me + k, count)}, device_id_type=MESH
        )
        return 0

    lax.fori_loop(1, count, greet, 0)
    pl.semaphore_wait(barrier, count - 1)

    def later(k):
        return pltpu.make_async_remote_copy(
            src_ref=totals.at[pl.ds(0, order)], dst_ref=held_a.at[me],
            send_sem=send_a.at[k], recv_sem=recv_a.at[me],
            device_id={"ctx": lax.rem(me + k, count)}, device_id_type=MESH,
        )

    def earlier(k):
        return pltpu.make_async_remote_copy(
            src_ref=totals.at[pl.ds(order, order)], dst_ref=held_b.at[me],
            send_sem=send_b.at[k], recv_sem=recv_b.at[me],
            device_id={"ctx": lax.rem(me + count - k, count)}, device_id_type=MESH,
        )

    def rim():
        return pltpu.make_async_remote_copy(
            src_ref=edge, dst_ref=held_e,
            send_sem=edge_sem.at[0], recv_sem=edge_sem.at[1],
            device_id={"ctx": lax.rem(me + count - 1, count)}, device_id_type=MESH,
        )

    @pl.when(me >= 1)
    def _():
        rim().start()

    def begin(k, _):
        @pl.when(me + k < count)
        def _():
            later(k).start()

        @pl.when(me >= k)
        def _():
            earlier(k).start()

        return 0

    lax.fori_loop(1, count, begin, 0)
    fall = jnp.exp(-rate[...])
    states[...] = jnp.zeros_like(states)
    next_edge[...] = jnp.zeros_like(next_edge)

    def add_a(src, _):
        pltpu.make_async_remote_copy(
            src_ref=totals.at[pl.ds(0, order)], dst_ref=held_a.at[src],
            send_sem=send_a.at[0], recv_sem=recv_a.at[src],
            device_id={"ctx": lax.rem(me + 1, count)}, device_id_type=MESH,
        ).wait_recv()
        states[0:order, :] = fall * states[0:order, :] + held_a[src]
        return 0

    def add_b(i, _):
        src = count - 1 - i
        pltpu.make_async_remote_copy(
            src_ref=totals.at[pl.ds(order, order)], dst_ref=held_b.at[src],
            send_sem=send_b.at[0], recv_sem=recv_b.at[src],
            device_id={"ctx": lax.rem(me + 1, count)}, device_id_type=MESH,
        ).wait_recv()
        states[order : 2 * order, :] = fall * states[order : 2 * order, :] + held_b[src]
        return 0

    lax.fori_loop(0, me, add_a, 0)
    lax.fori_loop(0, count - 1 - me, add_b, 0)

    @pl.when(me < count - 1)
    def _():
        rim().wait_recv()
        next_edge[...] = held_e[...]

    @pl.when(me >= 1)
    def _():
        rim().wait_send()

    def finish(k, _):
        @pl.when(me + k < count)
        def _():
            later(k).wait_send()

        @pl.when(me >= k)
        def _():
            earlier(k).wait_send()

        return 0

    lax.fori_loop(1, count, finish, 0)


def exchange(totals, edge, span_rate):
    count = lax.axis_size("ctx")
    order, chans = span_rate.shape
    dma = pltpu.SemaphoreType.DMA
    vmem = pl.BlockSpec(memory_space=pltpu.VMEM)
    return pl.pallas_call(
        lambda *refs: exchange_kernel(count, *refs),
        in_specs=[vmem] * 3,
        out_specs=[vmem] * 2,
        out_shape=[
            jax.ShapeDtypeStruct(totals.shape, F32),
            jax.ShapeDtypeStruct(edge.shape, F32),
        ],
        scratch_shapes=[pltpu.VMEM((count, order, chans), F32)] * 2
        + [pltpu.VMEM(edge.shape, F32)]
        + [dma((count,))] * 4
        + [dma((2,))],
        compiler_params=pltpu.CompilerParams(
            collective_id=0, has_side_effects=True, vmem_limit_bytes=32 * 2**20
        ),
    )(totals, edge, span_rate)


def total_kernel(dp_count, ctx_count, parts, result, held, totals, out_1, out_2, in_1, in_2):
    count = dp_count * ctx_count
    tiles = parts.shape[0]
    me = lax.axis_index("dp") * ctx_count + lax.axis_index("ctx")
    barrier = pltpu.get_barrier_semaphore()

    def place(rank):
        return {"dp": rank // ctx_count, "ctx": lax.rem(rank, ctx_count)}

    def when(always, cond, run):
        if always:
            run()
        else:
            pl.when(cond)(run)

    every = count == tiles

    def greet(k, _):
        pl.semaphore_signal(
            barrier, inc=1, device_id=place(lax.rem(me + k, count)), device_id_type=MESH
        )
        return 0

    lax.fori_loop(1, count, greet, 0)
    pl.semaphore_wait(barrier, count - 1)

    def part_copy(k, peer, source):
        return pltpu.make_async_remote_copy(
            src_ref=parts.at[peer], dst_ref=held.at[source],
            send_sem=out_1.at[k], recv_sem=in_1.at[source],
            device_id=place(lax.rem(me + k, count)), device_id_type=MESH,
        )

    def total_copy(k, source):
        return pltpu.make_async_remote_copy(
            src_ref=totals.at[source], dst_ref=totals.at[source],
            send_sem=out_2.at[k], recv_sem=in_2.at[source],
            device_id=place(lax.rem(me + k, count)), device_id_type=MESH,
        )

    def send_part(k, _):
        peer = lax.rem(me + k, count)
        when(every, peer < tiles, lambda: part_copy(k, peer, me).start())
        return 0

    lax.fori_loop(1, count, send_part, 0)

    def own():
        held[me] = parts[me]

        def arrive(k, _):
            part_copy(1, 0, lax.rem(me + k, count)).wait_recv()
            return 0

        lax.fori_loop(1, count, arrive, 0)

        def add(i, acc):
            return acc + held[i]

        totals[me] = lax.fori_loop(1, count, add, held[0])

        def send_total(k, _):
            total_copy(k, me).start()
            return 0

        lax.fori_loop(1, count, send_total, 0)

    when(every, me < tiles, own)

    def got(t, _):
        @pl.when(t != me)
        def _():
            total_copy(1, t).wait_recv()

        return 0

    lax.fori_loop(0, tiles, got, 0)
    result[...] = totals[...]

    def sent(k, _):
        peer = lax.rem(me + k, count)
        when(every, peer < tiles, lambda: part_copy(k, peer, me).wait_send())
        when(every, me < tiles, lambda: total_copy(k, me).wait_send())
        return 0

    lax.fori_loop(1, count, sent, 0)


def sum_all(parts):
    dp_count, ctx_count = lax.axis_size("dp"), lax.axis_size("ctx")
    count = dp_count * ctx_count
    if count < parts.shape[0]:
        return lax.psum(parts, ("dp", "ctx"))
    dma = pltpu.SemaphoreType.DMA
    vmem = pl.BlockSpec(memory_space=pltpu.VMEM)
    return pl.pallas_call(
        lambda *refs: total_kernel(dp_count, ctx_count, *refs),
        in_specs=[vmem],
        out_specs=vmem,
        out_shape=jax.ShapeDtypeStruct(parts.shape, F32),
        scratch_shapes=[
            pltpu.VMEM((count,) + parts.shape[1:], F32),
            pltpu.VMEM(parts.shape, F32),
            dma((count,)),
            dma((count,)),
            dma((count,)),
            dma((parts.shape[0],)),
        ],
        compiler_params=pltpu.CompilerParams(
            collective_id=1, has_side_effects=True, vmem_limit_bytes=32 * 2**20
        ),
    )(parts)


def on_device(projected, cotangent, short_filter, residues, decay_rate, skip_gain):
    proj = projected[0]
    _, chans, tokens = proj.shape
    order = residues.shape[1]
    span = tokens // SUBS
    tiles = chans // LANES
    pieces = lax.axis_size("tp")
    total_tokens = tokens * lax.axis_size("ctx") * lax.axis_size("dp")
    scale = 1.0 / math.sqrt(total_tokens)

    cot = cotangent[0].reshape(pieces, chans, tokens // pieces)
    cot = lax.all_to_all(cot, "tp", split_axis=0, concat_axis=0, tiled=True)
    rim = jnp.swapaxes(proj[:, :, tokens - 2 :], 1, 2).reshape(6, chans)
    rim = shifted(rim, 1).astype(F32)
    taps = short_filter.reshape(9, chans)
    rate = decay_rate.T
    res = residues.T
    gain = skip_gain[None]
    r = jnp.arange(tokens)
    perm = ((r % SUBS) * span + r // SUBS)[:, None] == r[None, :]
    perm_t = perm.T.astype(BF16)
    perm = perm.astype(BF16)
    ident = jnp.eye(LANES, dtype=BF16)

    def cols(*lead):
        zeros = (0,) * len(lead)
        return pl.BlockSpec(lead + (LANES,), lambda i: zeros + (i,))

    def whole(rows, columns):
        return pl.BlockSpec((rows, columns), lambda i: (0, 0))

    def chan_rows(lead, last):
        return pl.BlockSpec((lead, LANES, last), lambda i: (0, i, 0))

    params = pltpu.CompilerParams(
        dimension_semantics=("arbitrary",), vmem_limit_bytes=40 * 2**20
    )
    work = chans * tokens * order
    feat, inner, totals, edge = pl.pallas_call(
        first_kernel,
        grid=(tiles,),
        in_specs=[
            chan_rows(3, tokens),
            chan_rows(pieces, tokens // pieces),
            cols(6),
            cols(9),
            cols(order),
            whole(tokens, tokens),
        ],
        out_specs=[cols(4, tokens), cols(2 * order * SUBS), cols(2 * order), cols(8)],
        out_shape=[
            jax.ShapeDtypeStruct((4, tokens, chans), BF16),
            jax.ShapeDtypeStruct((2 * order * SUBS, chans), F32),
            jax.ShapeDtypeStruct((2 * order, chans), F32),
            jax.ShapeDtypeStruct((8, chans), F32),
        ],
        scratch_shapes=[pltpu.VMEM((tokens, LANES), F32)] * 2,
        compiler_params=params,
        cost_estimate=pl.CostEstimate(
            flops=4 * work, bytes_accessed=2**23, transcendentals=0
        ),
    )(proj, cot, rim, taps, rate, perm)

    states, next_edge = exchange(totals, edge, rate * float(tokens))

    out, grad_in, sums = pl.pallas_call(
        lambda *refs: second_kernel(scale, *refs),
        grid=(tiles,),
        in_specs=[
            cols(4, tokens),
            cols(2 * order * SUBS),
            cols(2 * order),
            cols(8),
            cols(9),
            cols(order),
            cols(order),
            cols(1),
            whole(tokens, tokens),
            whole(LANES, LANES),
        ],
        out_specs=[
            pl.BlockSpec((LANES, tokens), lambda i: (i, 0)),
            chan_rows(3, tokens),
            pl.BlockSpec((None, order + SUBS, LANES), lambda i: (i, 0, 0)),
        ],
        out_shape=[
            jax.ShapeDtypeStruct((chans, tokens), BF16),
            jax.ShapeDtypeStruct((3, chans, tokens), BF16),
            jax.ShapeDtypeStruct((tiles, order + SUBS, LANES), F32),
        ],
        scratch_shapes=[pltpu.VMEM((tokens, LANES), F32)] * 4
        + [pltpu.VMEM((order * SUBS, LANES), F32)] * 2
        + [pltpu.VMEM((order, LANES), F32)],
        compiler_params=params,
        cost_estimate=pl.CostEstimate(
            flops=12 * work, bytes_accessed=2**23, transcendentals=0
        ),
    )(feat, inner, states, next_edge, taps, rate, res, gain, perm_t, ident)
    sums = sum_all(sums)
    modes = jnp.swapaxes(sums[:, :order], 1, 2).reshape(chans, order)
    return (out[None], grad_in[None], modes, sums[:, order].reshape(chans))


def solution(mesh):
    placed = (
        P("dp", None, "tp", "ctx"),
        P("dp", None, ("ctx", "tp")),
        P(None, None, "tp"),
        P("tp", None),
        P("tp", None),
        P("tp"),
    )
    return jax.shard_map(
        on_device,
        mesh=mesh,
        in_specs=placed,
        out_specs=(P("dp", "tp", "ctx"), P("dp", None, "tp", "ctx"), P("tp", None), P("tp")),
        check_vma=False,
    )
```

```python
import math

import jax
import jax.numpy as jnp
import numpy as np
from jax import lax
from jax.experimental import pallas as pl
from jax.experimental.pallas import tpu as pltpu
from jax.sharding import PartitionSpec as P

LANES = 128
SUBS = 8
FOLD = 4
F32 = jnp.float32
BF16 = jnp.bfloat16


def rounded(values):
    return values.astype(BF16).astype(F32)


def nt_dot(left, right):
    return lax.dot_general(left, right, (((1,), (1,)), ((), ())), preferred_element_type=F32)


def row_of(ref, index):
    return jnp.broadcast_to(ref[index : index + 1, :], (SUBS, LANES))


def tree_sum(terms):
    terms = list(terms)
    while len(terms) > 1:
        paired = [terms[i] + terms[i + 1] for i in range(0, len(terms) - 1, 2)]
        if len(terms) % 2:
            paired.append(terms[-1])
        terms = paired
    return terms[0]


def sublane_ids():
    return lax.broadcasted_iota(jnp.int32, (SUBS, LANES), 0)


def scan_subs(ends, rate, span, sub, backward):
    running = ends
    step = 1
    while step < SUBS:
        if backward:
            moved = jnp.where(sub < SUBS - step, pltpu.roll(running, SUBS - step, 0), 0.0)
        else:
            moved = jnp.where(sub >= step, pltpu.roll(running, step, 0), 0.0)
        running = running + jnp.exp(-rate * float(span * step)) * moved
        step *= 2
    if backward:
        before = jnp.where(sub < SUBS - 1, pltpu.roll(running, SUBS - 1, 0), 0.0)
    else:
        before = jnp.where(sub >= 1, pltpu.roll(running, 1, 0), 0.0)
    return before, running


def folded(kernel, fold, axes):
    def run(*refs):
        for h in range(fold):
            views = []
            for ref, axis in zip(refs, axes):
                if axis is None:
                    views.append(ref)
                elif axis == "tile":
                    views.append(ref.at[h])
                else:
                    where = [slice(None)] * len(ref.shape)
                    where[axis] = pl.ds(h * LANES, LANES)
                    views.append(ref.at[tuple(where)])
            kernel(*views, *refs[len(axes) :])

    return run


def rim_kernel(proj, rim):
    width = proj.shape[2]
    row = lax.broadcasted_iota(jnp.int32, (SUBS, width), 0)
    column = lax.broadcasted_iota(jnp.int32, (SUBS, width), 1)
    total = None
    for s in range(3):
        pick = jnp.where((row // 2 == s) & (column == width - 2 + row % 2), 1.0, 0.0)
        part = nt_dot(pick.astype(BF16), proj[s])
        total = part if total is None else total + part
    rim[...] = total


def first_kernel(proj, cot, rim, taps, rate, perm, feat, inner, totals, edge, u_s, d_s):
    order = rate.shape[0]
    tokens = proj.shape[2]
    span = tokens // SUBS
    sub = sublane_ids()
    streams = []
    for s in range(3):
        rows = nt_dot(perm[...], proj[s])
        last = jnp.where(
            sub == 0, row_of(rim, 2 * s + 1), pltpu.roll(rows[tokens - SUBS :], 1, 0)
        )
        prior = jnp.where(
            sub == 0,
            row_of(rim, 2 * s),
            pltpu.roll(rows[tokens - 2 * SUBS : tokens - SUBS], 1, 0),
        )
        wide = jnp.concatenate([prior, last, rows], axis=0)
        made = taps[3 * s : 3 * s + 1, :] * rows
        made = made + taps[3 * s + 1 : 3 * s + 2, :] * wide[SUBS : SUBS + tokens]
        made = made + taps[3 * s + 2 : 3 * s + 3, :] * wide[:tokens]
        narrow = made.astype(BF16)
        feat[s] = narrow
        streams.append(narrow.astype(F32))
    pieces, part = cot.shape[0], cot.shape[2]
    grad = nt_dot(perm[:, :part], cot[0])
    for p in range(1, pieces):
        grad = grad + nt_dot(perm[:, p * part : (p + 1) * part], cot[p])
    feat[3] = grad.astype(BF16)
    streams.append(grad)
    for s in range(4):
        edge[2 * s : 2 * s + 1, :] = streams[s][0:1]
        edge[2 * s + 1 : 2 * s + 2, :] = streams[s][SUBS : SUBS + 1]
    u_s[...] = rounded(streams[1] * streams[2])
    d_s[...] = rounded(streams[3] * streams[0])
    falls = [jnp.exp(-row_of(rate, n)) for n in range(order)]

    def body(j, carry):
        ahead, back = carry
        uj = u_s[pl.ds(pl.multiple_of(j * SUBS, SUBS), SUBS), :]
        dj = d_s[pl.ds(pl.multiple_of((span - 1 - j) * SUBS, SUBS), SUBS), :]
        ahead = tuple(falls[n] * ahead[n] + uj for n in range(order))
        back = tuple(falls[n] * back[n] + dj for n in range(order))
        return ahead, back

    zero = jnp.zeros((SUBS, LANES), F32)
    ahead, back = lax.fori_loop(0, span, body, ((zero,) * order, (zero,) * order), unroll=4)
    for n in range(order):
        rate_n = row_of(rate, n)
        before, running = scan_subs(ahead[n], rate_n, span, sub, False)
        inner[n * SUBS : (n + 1) * SUBS, :] = before
        totals[n : n + 1, :] = running[SUBS - 1 : SUBS]
        before, running = scan_subs(back[n], rate_n, span, sub, True)
        inner[(order + n) * SUBS : (order + n + 1) * SUBS, :] = before
        totals[order + n : order + n + 1, :] = running[0:1]


def second_kernel(
    scale, feat, inner, states, edge, taps, rate, res, gain, perm_t, ident,
    out, grad_in, sums, u_s, d_s, z_s, b_s, a_s, w_s, x_s,
):
    order = rate.shape[0]
    tokens = feat.shape[1]
    span = tokens // SUBS
    sub = sublane_ids()
    sub_f = sub.astype(F32)
    root = jnp.sqrt(2.0 * rate[...])
    weight = res[...] * root
    fall = jnp.exp(-rate[...])
    for n in range(order):
        a_s[n * SUBS : (n + 1) * SUBS, :] = jnp.broadcast_to(fall[n : n + 1], (SUBS, LANES))
        w_s[n * SUBS : (n + 1) * SUBS, :] = jnp.broadcast_to(weight[n : n + 1], (SUBS, LANES))
    gain_b = jnp.broadcast_to(gain[...], (SUBS, LANES))
    u_s[...] = rounded(feat[1].astype(F32) * feat[2].astype(F32))
    d_s[...] = rounded(feat[3].astype(F32) * feat[0].astype(F32))

    def mode(ref, n):
        return ref[n * SUBS : (n + 1) * SUBS, :]

    def ahead_body(j, carry):
        xs, gs, skip = carry
        at = pl.ds(pl.multiple_of(j * SUBS, SUBS), SUBS)
        uj, dj = u_s[at, :], d_s[at, :]
        xs = tuple(mode(a_s, n) * xs[n] + uj for n in range(order))
        gs = tuple(gs[n] + dj * xs[n] for n in range(order))
        y = tree_sum([mode(w_s, n) * xs[n] for n in range(order)])
        z_s[at, :] = rounded(y + gain_b * uj)
        return xs, gs, skip + dj * uj

    zero = jnp.zeros((SUBS, LANES), F32)
    start = tuple(
        mode(inner, n) + jnp.exp(-row_of(rate, n) * (sub_f * float(span))) * row_of(states, n)
        for n in range(order)
    )
    xs, gs, skip = lax.fori_loop(
        0, span, ahead_body, (start, (zero,) * order, zero), unroll=4
    )
    for n in range(order):
        sums[n : n + 1, :] = jnp.sum(gs[n], axis=0, keepdims=True)
        x_s[n : n + 1, :] = xs[n][SUBS - 1 : SUBS]
    sums[0:order, :] = sums[0:order, :] * root * scale
    sums[order : order + SUBS, :] = jnp.broadcast_to(
        jnp.sum(skip, axis=0, keepdims=True) * scale, (SUBS, LANES)
    )

    def back_body(i, xs):
        at = pl.ds(pl.multiple_of((span - 1 - i) * SUBS, SUBS), SUBS)
        dj = d_s[at, :]
        xs = tuple(mode(a_s, n) * xs[n] + dj for n in range(order))
        y = tree_sum([mode(w_s, n) * xs[n] for n in range(order)])
        b_s[at, :] = rounded(y + gain_b * dj)
        return xs

    start = tuple(
        mode(inner, order + n)
        + jnp.exp(-row_of(rate, n) * ((SUBS - 1.0 - sub_f) * float(span)))
        * row_of(states, order + n)
        for n in range(order)
    )
    lax.fori_loop(0, span, back_body, start, unroll=4)

    gain_r = gain[...]
    q_n, k_n, v_n, g_n = (
        [edge[2 * s : 2 * s + 1, :], edge[2 * s + 1 : 2 * s + 2, :]] for s in range(4)
    )
    u_n = [rounded(k_n[i] * v_n[i]) for i in range(2)]
    d_n = [rounded(g_n[i] * q_n[i]) for i in range(2)]
    state = x_s[...]
    b_state = states[order : 2 * order, :]
    next_rows = []
    for i in range(2):
        state = fall * state + u_n[i]
        z_n = rounded(jnp.sum(weight * state, axis=0, keepdims=True) + gain_r * u_n[i])
        if i:
            b_state = (b_state - d_n[i - 1]) / fall
        du_n = rounded(jnp.sum(weight * b_state, axis=0, keepdims=True) + gain_r * d_n[i])
        next_rows.append(
            [rounded(g_n[i] * z_n), rounded(du_n * v_n[i]), rounded(du_n * k_n[i])]
        )

    def send_out(rows):
        ordered = jnp.dot(perm_t[...], rows, preferred_element_type=F32).astype(BF16)
        return nt_dot(ident[...], ordered).astype(BF16)

    z = z_s[...]
    du = b_s[...]
    out[...] = send_out((feat[0].astype(F32) * z).astype(BF16))
    for s in range(3):
        if s == 0:
            rows = rounded(feat[3].astype(F32) * z)
        else:
            rows = rounded(du * feat[3 - s].astype(F32))
        after = [
            jnp.where(
                sub == SUBS - 1,
                jnp.broadcast_to(next_rows[i][s], (SUBS, LANES)),
                pltpu.roll(rows[i * SUBS : (i + 1) * SUBS], SUBS - 1, 0),
            )
            for i in range(2)
        ]
        wide = jnp.concatenate([rows] + after, axis=0)
        made = taps[3 * s : 3 * s + 1, :] * rows
        made = made + taps[3 * s + 1 : 3 * s + 2, :] * wide[SUBS : SUBS + tokens]
        made = made + taps[3 * s + 2 : 3 * s + 3, :] * wide[2 * SUBS :]
        grad_in[s] = send_out(made.astype(BF16))


def shifted(array, by):
    count = lax.axis_size("ctx")
    pairs = [(i, i + by) for i in range(count) if 0 <= i + by < count]
    return lax.ppermute(array, "ctx", pairs)


MESH = pl.DeviceIdType.MESH


def exchange_kernel(count, totals, edge, rate, states, next_edge, held_a, held_b, held_e,
                    send_a, send_b, recv_a, recv_b, edge_sem):
    order = rate.shape[0]
    me = lax.axis_index("ctx")
    barrier = pltpu.get_barrier_semaphore()

    def greet(k, _):
        pl.semaphore_signal(
            barrier, inc=1, device_id={"ctx": lax.rem(me + k, count)}, device_id_type=MESH
        )
        return 0

    lax.fori_loop(1, count, greet, 0)
    pl.semaphore_wait(barrier, count - 1)

    def later(k):
        return pltpu.make_async_remote_copy(
            src_ref=totals.at[pl.ds(0, order)], dst_ref=held_a.at[me],
            send_sem=send_a.at[k], recv_sem=recv_a.at[me],
            device_id={"ctx": lax.rem(me + k, count)}, device_id_type=MESH,
        )

    def earlier(k):
        return pltpu.make_async_remote_copy(
            src_ref=totals.at[pl.ds(order, order)], dst_ref=held_b.at[me],
            send_sem=send_b.at[k], recv_sem=recv_b.at[me],
            device_id={"ctx": lax.rem(me + count - k, count)}, device_id_type=MESH,
        )

    def rim():
        return pltpu.make_async_remote_copy(
            src_ref=edge, dst_ref=held_e,
            send_sem=edge_sem.at[0], recv_sem=edge_sem.at[1],
            device_id={"ctx": lax.rem(me + count - 1, count)}, device_id_type=MESH,
        )

    @pl.when(me >= 1)
    def _():
        rim().start()

    def begin(k, _):
        @pl.when(me + k < count)
        def _():
            later(k).start()

        @pl.when(me >= k)
        def _():
            earlier(k).start()

        return 0

    lax.fori_loop(1, count, begin, 0)
    fall = jnp.exp(-rate[...])
    states[...] = jnp.zeros_like(states)
    next_edge[...] = jnp.zeros_like(next_edge)

    def add_a(src, _):
        pltpu.make_async_remote_copy(
            src_ref=totals.at[pl.ds(0, order)], dst_ref=held_a.at[src],
            send_sem=send_a.at[0], recv_sem=recv_a.at[src],
            device_id={"ctx": lax.rem(me + 1, count)}, device_id_type=MESH,
        ).wait_recv()
        states[0:order, :] = fall * states[0:order, :] + held_a[src]
        return 0

    def add_b(i, _):
        src = count - 1 - i
        pltpu.make_async_remote_copy(
            src_ref=totals.at[pl.ds(order, order)], dst_ref=held_b.at[src],
            send_sem=send_b.at[0], recv_sem=recv_b.at[src],
            device_id={"ctx": lax.rem(me + 1, count)}, device_id_type=MESH,
        ).wait_recv()
        states[order : 2 * order, :] = fall * states[order : 2 * order, :] + held_b[src]
        return 0

    lax.fori_loop(0, me, add_a, 0)
    lax.fori_loop(0, count - 1 - me, add_b, 0)

    @pl.when(me < count - 1)
    def _():
        rim().wait_recv()
        next_edge[...] = held_e[...]

    @pl.when(me >= 1)
    def _():
        rim().wait_send()

    def finish(k, _):
        @pl.when(me + k < count)
        def _():
            later(k).wait_send()

        @pl.when(me >= k)
        def _():
            earlier(k).wait_send()

        return 0

    lax.fori_loop(1, count, finish, 0)


def exchange(totals, edge, span_rate):
    count = lax.axis_size("ctx")
    order, chans = span_rate.shape
    dma = pltpu.SemaphoreType.DMA
    vmem = pl.BlockSpec(memory_space=pltpu.VMEM)
    return pl.pallas_call(
        lambda *refs: exchange_kernel(count, *refs),
        in_specs=[vmem] * 3,
        out_specs=[vmem] * 2,
        out_shape=[
            jax.ShapeDtypeStruct(totals.shape, F32),
            jax.ShapeDtypeStruct(edge.shape, F32),
        ],
        scratch_shapes=[pltpu.VMEM((count, order, chans), F32)] * 2
        + [pltpu.VMEM(edge.shape, F32)]
        + [dma((count,))] * 4
        + [dma((2,))],
        compiler_params=pltpu.CompilerParams(
            collective_id=0, has_side_effects=True, vmem_limit_bytes=32 * 2**20
        ),
    )(totals, edge, span_rate)


def total_kernel(dp_count, ctx_count, parts, result, held, totals, out_1, out_2, in_1, in_2):
    count = dp_count * ctx_count
    tiles = parts.shape[0]
    me = lax.axis_index("dp") * ctx_count + lax.axis_index("ctx")
    barrier = pltpu.get_barrier_semaphore()

    def place(rank):
        return {"dp": rank // ctx_count, "ctx": lax.rem(rank, ctx_count)}

    def when(always, cond, run):
        if always:
            run()
        else:
            pl.when(cond)(run)

    every = count == tiles

    def greet(k, _):
        pl.semaphore_signal(
            barrier, inc=1, device_id=place(lax.rem(me + k, count)), device_id_type=MESH
        )
        return 0

    lax.fori_loop(1, count, greet, 0)
    pl.semaphore_wait(barrier, count - 1)

    def part_copy(k, peer, source):
        return pltpu.make_async_remote_copy(
            src_ref=parts.at[peer], dst_ref=held.at[source],
            send_sem=out_1.at[k], recv_sem=in_1.at[source],
            device_id=place(lax.rem(me + k, count)), device_id_type=MESH,
        )

    def total_copy(k, source):
        return pltpu.make_async_remote_copy(
            src_ref=totals.at[source], dst_ref=totals.at[source],
            send_sem=out_2.at[k], recv_sem=in_2.at[source],
            device_id=place(lax.rem(me + k, count)), device_id_type=MESH,
        )

    def send_part(k, _):
        peer = lax.rem(me + k, count)
        when(every, peer < tiles, lambda: part_copy(k, peer, me).start())
        return 0

    lax.fori_loop(1, count, send_part, 0)

    def own():
        held[me] = parts[me]

        def arrive(k, _):
            part_copy(1, 0, lax.rem(me + k, count)).wait_recv()
            return 0

        lax.fori_loop(1, count, arrive, 0)

        def add(i, acc):
            return acc + held[i]

        totals[me] = lax.fori_loop(1, count, add, held[0])

        def send_total(k, _):
            total_copy(k, me).start()
            return 0

        lax.fori_loop(1, count, send_total, 0)

    when(every, me < tiles, own)

    def got(t, _):
        @pl.when(t != me)
        def _():
            total_copy(1, t).wait_recv()

        return 0

    lax.fori_loop(0, tiles, got, 0)
    result[...] = totals[...]

    def sent(k, _):
        peer = lax.rem(me + k, count)
        when(every, peer < tiles, lambda: part_copy(k, peer, me).wait_send())
        when(every, me < tiles, lambda: total_copy(k, me).wait_send())
        return 0

    lax.fori_loop(1, count, sent, 0)


def sum_all(parts):
    dp_count, ctx_count = lax.axis_size("dp"), lax.axis_size("ctx")
    count = dp_count * ctx_count
    if count < parts.shape[0]:
        return lax.psum(parts, ("dp", "ctx"))
    dma = pltpu.SemaphoreType.DMA
    vmem = pl.BlockSpec(memory_space=pltpu.VMEM)
    return pl.pallas_call(
        lambda *refs: total_kernel(dp_count, ctx_count, *refs),
        in_specs=[vmem],
        out_specs=vmem,
        out_shape=jax.ShapeDtypeStruct(parts.shape, F32),
        scratch_shapes=[
            pltpu.VMEM((count,) + parts.shape[1:], F32),
            pltpu.VMEM(parts.shape, F32),
            dma((count,)),
            dma((count,)),
            dma((count,)),
            dma((parts.shape[0],)),
        ],
        compiler_params=pltpu.CompilerParams(
            collective_id=1, has_side_effects=True, vmem_limit_bytes=32 * 2**20
        ),
    )(parts)


def on_device(projected, cotangent, short_filter, residues, decay_rate, skip_gain):
    proj = projected[0]
    _, chans, tokens = proj.shape
    order = residues.shape[1]
    span = tokens // SUBS
    tiles = chans // LANES
    pieces = lax.axis_size("tp")
    total_tokens = tokens * lax.axis_size("ctx") * lax.axis_size("dp")
    scale = 1.0 / math.sqrt(total_tokens)

    cot = cotangent[0].reshape(pieces, chans, tokens // pieces)
    cot = lax.all_to_all(cot, "tp", split_axis=0, concat_axis=0, tiled=True)
    last_lanes = math.gcd(tokens, LANES)
    rim = pl.pallas_call(
        rim_kernel,
        grid=(1,),
        in_specs=[
            pl.BlockSpec((3, chans, last_lanes), lambda i: (0, 0, tokens // last_lanes - 1))
        ],
        out_specs=pl.BlockSpec((SUBS, chans), lambda i: (0, 0)),
        out_shape=jax.ShapeDtypeStruct((SUBS, chans), F32),
        compiler_params=pltpu.CompilerParams(vmem_limit_bytes=24 * 2**20),
        cost_estimate=pl.CostEstimate(flops=2**24, bytes_accessed=2**21, transcendentals=0),
    )(proj)
    rim = shifted(rim, 1)
    taps = short_filter.reshape(9, chans)
    rate = decay_rate.T
    res = residues.T
    gain = skip_gain[None]
    r = np.arange(tokens)
    order_of = ((r % SUBS) * span + r // SUBS)[:, None] == r[None, :]
    perm = jnp.asarray(order_of.astype(BF16))
    perm_t = jnp.asarray(order_of.T.astype(BF16))
    ident = jnp.asarray(np.eye(LANES).astype(BF16))
    fold = math.gcd(FOLD, tiles)
    block = fold * LANES

    def cols(*lead):
        zeros = (0,) * len(lead)
        return pl.BlockSpec(lead + (block,), lambda i: zeros + (i,))

    def whole(rows, columns):
        return pl.BlockSpec((rows, columns), lambda i: (0, 0))

    def chan_rows(lead, last):
        return pl.BlockSpec((lead, block, last), lambda i: (0, i, 0))

    params = pltpu.CompilerParams(
        dimension_semantics=("arbitrary",), vmem_limit_bytes=40 * 2**20
    )
    work = chans * tokens * order
    feat, inner, totals, edge = pl.pallas_call(
        folded(first_kernel, fold, [1, 1, 1, 1, 1, None, 2, 1, 1, 1]),
        grid=(tiles // fold,),
        in_specs=[
            chan_rows(3, tokens),
            chan_rows(pieces, tokens // pieces),
            cols(SUBS),
            cols(9),
            cols(order),
            whole(tokens, tokens),
        ],
        out_specs=[cols(4, tokens), cols(2 * order * SUBS), cols(2 * order), cols(8)],
        out_shape=[
            jax.ShapeDtypeStruct((4, tokens, chans), BF16),
            jax.ShapeDtypeStruct((2 * order * SUBS, chans), F32),
            jax.ShapeDtypeStruct((2 * order, chans), F32),
            jax.ShapeDtypeStruct((8, chans), F32),
        ],
        scratch_shapes=[pltpu.VMEM((tokens, LANES), F32)] * 2,
        compiler_params=params,
        cost_estimate=pl.CostEstimate(
            flops=4 * work, bytes_accessed=2**23, transcendentals=0
        ),
    )(proj, cot, rim, taps, rate, perm)

    states, next_edge = exchange(totals, edge, rate * float(tokens))

    out, grad_in, sums = pl.pallas_call(
        folded(
            lambda *refs: second_kernel(scale, *refs),
            fold,
            [2, 1, 1, 1, 1, 1, 1, 1, None, None, 0, 1, "tile"],
        ),
        grid=(tiles // fold,),
        in_specs=[
            cols(4, tokens),
            cols(2 * order * SUBS),
            cols(2 * order),
            cols(8),
            cols(9),
            cols(order),
            cols(order),
            cols(1),
            whole(tokens, tokens),
            whole(LANES, LANES),
        ],
        out_specs=[
            pl.BlockSpec((block, tokens), lambda i: (i, 0)),
            chan_rows(3, tokens),
            pl.BlockSpec((fold, order + SUBS, LANES), lambda i: (i, 0, 0)),
        ],
        out_shape=[
            jax.ShapeDtypeStruct((chans, tokens), BF16),
            jax.ShapeDtypeStruct((3, chans, tokens), BF16),
            jax.ShapeDtypeStruct((tiles, order + SUBS, LANES), F32),
        ],
        scratch_shapes=[pltpu.VMEM((tokens, LANES), F32)] * 4
        + [pltpu.VMEM((order * SUBS, LANES), F32)] * 2
        + [pltpu.VMEM((order, LANES), F32)],
        compiler_params=params,
        cost_estimate=pl.CostEstimate(
            flops=12 * work, bytes_accessed=2**23, transcendentals=0
        ),
    )(feat, inner, states, next_edge, taps, rate, res, gain, perm_t, ident)
    sums = sum_all(sums)
    modes = jnp.swapaxes(sums[:, :order], 1, 2).reshape(chans, order)
    return (out[None], grad_in[None], modes, sums[:, order].reshape(chans))


def solution(mesh):
    placed = (
        P("dp", None, "tp", "ctx"),
        P("dp", None, ("ctx", "tp")),
        P(None, None, "tp"),
        P("tp", None),
        P("tp", None),
        P("tp"),
    )
    return jax.shard_map(
        on_device,
        mesh=mesh,
        in_specs=placed,
        out_specs=(P("dp", "tp", "ctx"), P("dp", None, "tp", "ctx"), P("tp", None), P("tp")),
        check_vma=False,
    )
```
